32 devices in a mesh: row: 4 (over y, x), col: 8 (over z, core).
Axes of the slice: x: 2, y: 2, z: 4, core: 2. Of those that a mesh axis runs over, the one named last changes fastest.
Arguments:
- kernel_blocks: bfloat16 [64, 4, 256, 256], P('col', 'row'), may hold values from -6 to 6
- row_intersection: bfloat16 [512, 256, 256], P('col'), may hold values from -0.375 to 0.375
- col_intersection: bfloat16 [16, 256, 256], P('row'), may hold values from -0.375 to 0.375
- trial: bfloat16 [16, 64, 256], P('row', 'col'), may hold values from -0.09375 to 0.09375
- coarse_of_row: int32 [512], replicated, may hold values from 0 to 63, as said below
Outputs:
- fine_kernel: bfloat16 [512, 16, 256, 256], P('col', 'row')
- applied: bfloat16 [512, 64, 256], P(('col', 'row'))
The draws below stay inside these ranges and needn't reach their ends.
Inputs may be any that keep to these rules, and one draw needn't show every extreme that they name: coarse_of_row never falls from one fine point to the next; coarse point 0 starts at fine point 0, and coarse point j >= 1 starts at fine point j * 8 - 512 // 128 + e_j with e_j between -3 and 3; every coarse point takes 1 to 15 consecutive fine points, and the last takes exactly 15.
All inputs are finite; a program needn't handle non-finite values.
Results may differ from the reference program's by a relative error of at most 0.0057.
Values may be sent and summed in bfloat16 or wider, within the bound.
No kernel may reach another device: no remote copies, remote signals or barrier semaphores. Data moves between devices by JAX's collectives and lax.ppermute only.
A program may use at most 128 MiB of HBM per device.

```python
import jax
import jax.numpy as jnp
from jax import lax

NK = 512
P_SIZE = 256
NV = 64
NC = 64
COLS_DEV = 4
CW = 4
COLS = 16


def draw_coarse_of_row(key, part):
    spacing = NK // NC
    jitter = jax.random.randint(jax.random.fold_in(key, 7), (NC,), -3, 4).astype(jnp.int32)
    jitter = jitter.at[NC - 1].set(-3)
    points = jnp.arange(NC, dtype=jnp.int32)
    starts = points * spacing - spacing // 2 + jitter
    starts = starts[1:]
    fine = jnp.arange(NK, dtype=jnp.int32)
    return jnp.sum((fine[:, None] >= starts[None, :]).astype(jnp.int32), axis=1).astype(jnp.int32)


def level_of(rng, extent, shards, smallest, high):
    gain, own = 1.0, jax.random.fold_in(rng, 6)
    for position, shards_of in shards:
        steps = jnp.exp(jax.random.uniform(jax.random.fold_in(own, position), (shards_of,), jnp.float32, smallest / len(shards), high / len(shards)))
        gain = gain * jnp.repeat(steps, extent[position] // shards_of).reshape([-1 if axis == position else 1 for axis in range(len(extent))])
    return gain


def bell_draw(key, extent, deviation, reach, cuts=(), held_as=jnp.bfloat16):
    values = deviation * jax.random.normal(key, extent, jnp.float32)
    if cuts:
        values = values * level_of(key, extent, cuts, -0.22, 0.18)
    return jnp.clip(values, -reach, reach).astype(held_as)


def setup_inputs(seed: int = 0) -> dict:
    splits = jax.random.split(jax.random.key(seed), 6)
    return {
        "kernel_blocks": bell_draw(splits[0], (NC, CW, P_SIZE, P_SIZE), 1.0, 6.0, ((0, 8), (1, 4))),
        "row_intersection": bell_draw(splits[1], (NK, P_SIZE, P_SIZE), P_SIZE ** -0.5, 0.375, ((0, 8),)),
        "col_intersection": bell_draw(splits[2], (COLS, P_SIZE, P_SIZE), P_SIZE ** -0.5, 0.375, ((0, 4),)),
        "trial": bell_draw(splits[3], (COLS, NV, P_SIZE), (COLS * P_SIZE) ** -0.5, 0.09375, ((0, 4), (1, 8))),
        "coarse_of_row": draw_coarse_of_row(jax.random.fold_in(splits[5], 71), 0),
    }


def reference(kernel_blocks, row_intersection, col_intersection, trial, coarse_of_row):
    intersection_wide = col_intersection.astype(jnp.float32)
    trial_wide = trial.astype(jnp.float32)

    def right_of(block_row):
        spread = jnp.repeat(block_row, COLS_DEV, axis=0).astype(jnp.float32)
        return jnp.einsum("jab,jbc->jac", spread, intersection_wide).astype(jnp.bfloat16)

    right_all = lax.map(right_of, kernel_blocks)

    def one_row(items):
        index, urow = items
        picked = lax.dynamic_index_in_dim(right_all, index.astype(jnp.int32), 0, keepdims=False).astype(jnp.float32)
        fine = jnp.einsum("ba,jbc->jac", urow.astype(jnp.float32), picked).astype(jnp.bfloat16)
        part = jnp.einsum("jab,jvb->va", fine.astype(jnp.float32), trial_wide).astype(jnp.bfloat16)
        return fine, part

    fine_kernel, applied = lax.map(one_row, (coarse_of_row, row_intersection))
    return fine_kernel, applied
```

```python
import functools

import jax
import jax.numpy as jnp
from jax import lax
from jax.experimental import pallas as pl
from jax.experimental.pallas import tpu as pltpu
from jax.sharding import PartitionSpec as P

BF = jnp.bfloat16
F32 = jnp.float32
MIB = 1024 * 1024
NT = (((1,), (1,)), ((), ()))
NN = (((1,), (0,)), ((), ()))


def dot(x, y, dims=NN):
    return lax.dot_general(x, y, dims, preferred_element_type=F32)


def two_terms(x):
    high = x.astype(BF)
    low = (x - high.astype(F32)).astype(BF)
    return jnp.concatenate([high, low], axis=0)


def folded_dot(x, y, dims=NN):
    z = dot(x, y, dims)
    half = z.shape[0] // 2
    return z[:half] + z[half:]


def rows_kernel(spacing, per, coarse, c_ref, k_ref, f_ref, u_ref, _, out, r_v, o_v, osem):
    nc = k_ref.shape[0]
    m = c_ref.shape[0]
    base_j = lax.axis_index("col") * nc
    base_k = lax.axis_index("col") * nc * spacing

    def right(j, block):
        for q in range(m):
            r_v[j, q] = dot(block, c_ref[q]).astype(BF)

    def write(k):
        return pltpu.make_async_copy(o_v.at[k], out.at[k], osem.at[k])

    def rows(i):
        for t in range(per * spacing):
            k = i * spacing + t
            at = jnp.clip(coarse[base_k + k] - base_j, 0, nc)
            ut = u_ref[k].T
            for q in range(m):
                o_v[k, q] = dot(ut, r_v[at, q]).astype(BF)
            write(k).start()

    right(nc, f_ref[0, 0])
    for j in range(min(per + 1, nc)):
        right(j, k_ref[j, 0])

    def step(n, carry):
        rows(n * per)
        for j in range(per):
            ahead = jnp.minimum(n * per + per + 1 + j, nc - 1)
            right(ahead, k_ref[ahead, 0])
        return carry

    lax.fori_loop(0, nc // per - 1, step, 0)
    rows(nc - per)
    for k in range(nc * spacing):
        write(k).wait()


def fine_rows(spacing, coarse, c, kb, following, u, after):
    rows, p, _ = u.shape
    nc, m = kb.shape[0], c.shape[0]
    per = 2 if nc % 2 == 0 else 1
    vmem = pl.BlockSpec(memory_space=pltpu.VMEM)
    return pl.pallas_call(
        functools.partial(rows_kernel, spacing, per),
        out_shape=jax.ShapeDtypeStruct((rows, m, p, p), BF),
        in_specs=[pl.BlockSpec(memory_space=pltpu.SMEM)] + [vmem] * 4 + [pl.BlockSpec(memory_space=pl.ANY)],
        out_specs=pl.BlockSpec(memory_space=pl.ANY),
        scratch_shapes=[
            pltpu.VMEM((nc + 1, m, p, p), BF),
            pltpu.VMEM((rows, m, p, p), BF),
            pltpu.SemaphoreType.DMA((rows,)),
        ],
        compiler_params=pltpu.CompilerParams(vmem_limit_bytes=50 * MIB),
        cost_estimate=pl.CostEstimate(
            flops=2 * rows * m * p**3, bytes_accessed=2 * rows * (m + 1) * p * p, transcendentals=0
        ),
        name="fine_rows",
    )(coarse, c, kb, following, u, after)


def shares_kernel(lows, n_row, n_col, c_ref, k_ref, f_ref, t_ref, own_ref, *refs):
    sends, w_v = refs[: n_row - 1], refs[-1]
    m, nv = t_ref.shape[:2]
    nc = k_ref.shape[0]
    s = two_terms(sum(dot(t_ref[q], c_ref[q], NT) for q in range(m)))
    each, half = nv // n_col, n_col // 2
    at = lax.broadcasted_iota(jnp.int32, (nv, nv), 1)
    block = lax.div(at, each)
    source = lax.bitwise_xor(lax.axis_index("col"), 2 * lax.rem(block, half) + lax.div(block, half))
    place = source * each + lax.rem(at, each)
    order = (place == lax.broadcasted_iota(jnp.int32, (nv, nv), 0)).astype(F32).astype(BF)
    s = jnp.concatenate([dot(order, s[:nv]), dot(order, s[nv:])], axis=0).astype(BF)
    for j in range(nc + 1):
        w_v[j] = folded_dot(s, k_ref[j, 0] if j < nc else f_ref[0, 0], NT)
    me = lax.axis_index("row")
    (own, spacing), width = lows
    own_ref[...] = w_v[pl.ds(me * own // spacing, width)]
    for n in range(1, n_row):
        other = lax.bitwise_xor(me, n)
        sends[n - 1][...] = w_v[pl.ds(other * own // spacing, width)].astype(BF)


def shares(lows, n_row, n_col, c, kb, following, t):
    nv, p = t.shape[1:]
    width = lows[1]
    vmem = pl.BlockSpec(memory_space=pltpu.VMEM)
    return pl.pallas_call(
        functools.partial(shares_kernel, lows, n_row, n_col),
        out_shape=[jax.ShapeDtypeStruct((width, nv, p), F32)]
        + [jax.ShapeDtypeStruct((width, nv, p), BF)] * (n_row - 1),
        in_specs=[vmem] * 4,
        out_specs=[vmem] * n_row,
        scratch_shapes=[pltpu.VMEM((kb.shape[0] + 1, nv, p), F32)],
        compiler_params=pltpu.CompilerParams(vmem_limit_bytes=16 * MIB),
        name="row_shares",
    )(c, kb, following, t)


def applied_kernel(lows, n_row, nc, spacing, coarse, u_ref, own_ref, *refs):
    got = refs[: n_row - 1]
    out, w_v = refs[-2:]
    (own, _), width = lows
    me = lax.axis_index("row")
    base_j = lax.axis_index("col") * nc + me * own // spacing
    base_k = lax.axis_index("col") * nc * spacing + me * own
    w = own_ref[...]
    for ref in got:
        w = w + ref[...].astype(F32)
    for i in range(width):
        w_v[i] = two_terms(w[i])
    for t in range(own):
        at = jnp.clip(coarse[base_k + t] - base_j, 0, width - 1)
        out[t] = folded_dot(w_v[at], u_ref[me * own + t]).astype(BF)


def applied_rows(lows, n_row, nc, spacing, coarse, u, own_share, got, after):
    width, nv, p = own_share.shape
    vmem = pl.BlockSpec(memory_space=pltpu.VMEM)
    return pl.pallas_call(
        functools.partial(applied_kernel, lows, n_row, nc, spacing),
        out_shape=jax.ShapeDtypeStruct((lows[0][0], nv, p), BF),
        in_specs=[pl.BlockSpec(memory_space=pltpu.SMEM)] + [vmem] * (n_row + 1),
        out_specs=vmem,
        scratch_shapes=[pltpu.VMEM((width, 2 * nv, p), BF)],
        compiler_params=pltpu.CompilerParams(vmem_limit_bytes=24 * MIB),
        name="applied_rows",
    )(coarse, u, own_share, *got)


def gather_trial(trial):
    n = lax.axis_size("col")

    def swap(x, by):
        return lax.ppermute(x, "col", [(i, i ^ by) for i in range(n)])

    half = jnp.concatenate([trial] + [swap(trial, by) for by in range(2, n, 2)], axis=1)
    return jnp.concatenate([half, swap(half, 1)], axis=1)


def per_device(kb, u, c, trial, coarse):
    n_row, n_col = lax.axis_size("row"), lax.axis_size("col")
    nc, rows = kb.shape[0], u.shape[0]
    spacing = rows // nc
    own = rows // n_row
    width = max((r * own + own - 1) // spacing + 2 - r * own // spacing for r in range(n_row))
    lows = ((own, spacing), width)
    full = gather_trial(trial)
    following = lax.ppermute(kb[0:1], "col", [(i + 1, i) for i in range(n_col - 1)])
    own_share, *sends = shares(lows, n_row, n_col, c, kb, following, full)
    got = [lax.ppermute(x, "row", [(i, i ^ (n + 1)) for i in range(n_row)]) for n, x in enumerate(sends)]
    fine = fine_rows(spacing, coarse, c, kb, following, u, own_share)
    applied = applied_rows(lows, n_row, nc, spacing, coarse, u, own_share, got, fine)
    return fine, applied


def solution(mesh):
    in_specs = (
        P("col", "row", None, None),
        P("col", None, None),
        P("row", None, None),
        P("row", "col", None),
        P(),
    )
    out_specs = (P("col", "row", None, None), P(("col", "row"), None, None))
    return jax.shard_map(
        per_device, mesh=mesh, in_specs=in_specs, out_specs=out_specs, check_vma=False
    )
```

```python
import functools

import jax
import jax.numpy as jnp
from jax import lax
from jax.experimental import pallas as pl
from jax.experimental.pallas import tpu as pltpu
from jax.sharding import PartitionSpec as P

BF = jnp.bfloat16
F32 = jnp.float32
MIB = 1024 * 1024
NT = (((1,), (1,)), ((), ()))
NN = (((1,), (0,)), ((), ()))


def dot(x, y, dims=NN):
    return lax.dot_general(x, y, dims, preferred_element_type=F32)


def two_terms(x):
    high = x.astype(BF)
    low = (x - high.astype(F32)).astype(BF)
    return jnp.concatenate([high, low], axis=0)


def folded_dot(x, y, dims=NN):
    z = dot(x, y, dims)
    half = z.shape[0] // 2
    return z[:half] + z[half:]


def ready_kernel(spacing, c_hbm, k_hbm, u_hbm, t_hbm, coarse_hbm, c_v, k_v, u_v, t_v, coarse_v, first_v, r_v, csem, tsem, osem, ksem, usem):
    nc = k_hbm.shape[0]

    def load_k(j):
        return pltpu.make_async_copy(k_hbm.at[j, 0], k_v.at[j], ksem.at[j])

    def load_u(j):
        here = pl.ds(j * spacing, spacing)
        return pltpu.make_async_copy(u_hbm.at[here], u_v.at[here], usem.at[j])

    small = [
        pltpu.make_async_copy(c_hbm, c_v, csem),
        pltpu.make_async_copy(t_hbm, t_v, tsem),
        pltpu.make_async_copy(coarse_hbm, coarse_v, osem),
    ]
    small[0].start()
    for j in range(nc):
        load_k(j).start()
    small[1].start()
    small[2].start()
    for j in range(nc):
        load_u(j).start()
    small[0].wait()
    for j in range(nc):
        load_k(j).wait()
    first_v[0] = k_v[0]
    for j in range(nc):
        for q in range(c_v.shape[0]):
            r_v[j, q] = dot(k_v[j], c_v[q]).astype(BF)
    for load in small[1:]:
        load.wait()
    for j in range(nc):
        load_u(j).wait()


def ready(spacing, c, kb, u, trial, coarse):
    nc, _, p, _ = kb.shape
    m = c.shape[0]
    vmem = pl.BlockSpec(memory_space=pltpu.VMEM)
    return pl.pallas_call(
        functools.partial(ready_kernel, spacing),
        out_shape=[
            jax.ShapeDtypeStruct(c.shape, BF),
            jax.ShapeDtypeStruct((nc, p, p), BF),
            jax.ShapeDtypeStruct(u.shape, BF),
            jax.ShapeDtypeStruct(trial.shape, BF),
            jax.ShapeDtypeStruct(coarse.shape, jnp.int32),
            jax.ShapeDtypeStruct((1, p, p), BF),
            jax.ShapeDtypeStruct((nc, m, p, p), BF),
        ],
        in_specs=[pl.BlockSpec(memory_space=pl.ANY)] * 5,
        out_specs=[vmem] * 7,
        scratch_shapes=[pltpu.SemaphoreType.DMA] * 3 + [pltpu.SemaphoreType.DMA((nc,))] * 2,
        compiler_params=pltpu.CompilerParams(vmem_limit_bytes=32 * MIB),
        cost_estimate=pl.CostEstimate(
            flops=20 * nc * m * p**3, bytes_accessed=2 * kb.size, transcendentals=0
        ),
        name="ready",
    )(c, kb, u, trial, coarse)


def rows_kernel(spacing, per, coarse_ref, c_ref, f_ref, r_ref, u_ref, _, out, r_v, o_v, coarse, csem, osem):
    nc, m = r_ref.shape[:2]
    base_j = lax.axis_index("col") * nc
    base_k = lax.axis_index("col") * nc * spacing
    load = pltpu.make_async_copy(coarse_ref, coarse, csem)
    load.start()

    def write(k):
        return pltpu.make_async_copy(o_v.at[k], out.at[k], osem.at[k])

    def rows(i, tail):
        for t in range(per * spacing):
            k = i * spacing + t
            at = coarse[base_k + k] - base_j
            ut = u_ref[k].T
            for q in range(m):
                if tail:
                    block = r_v[jnp.clip(at - (nc - per), 0, per), q]
                else:
                    block = r_ref[jnp.clip(at, 0, nc - 1), q]
                o_v[k, q] = dot(ut, block).astype(BF)
            write(k).start()

    for q in range(m):
        r_v[per, q] = dot(f_ref[0], c_ref[q]).astype(BF)
    for j in range(per):
        r_v[j] = r_ref[nc - per + j]
    load.wait()

    def step(n, carry):
        rows(n * per, False)
        return carry

    lax.fori_loop(0, nc // per - 1, step, 0)
    rows(nc - per, True)
    for k in range(nc * spacing):
        write(k).wait()


def fine_rows(spacing, coarse, c, following, right, u, after):
    rows, p, _ = u.shape
    nc, m = right.shape[:2]
    per = 1
    vmem = pl.BlockSpec(memory_space=pltpu.VMEM)
    return pl.pallas_call(
        functools.partial(rows_kernel, spacing, per),
        out_shape=jax.ShapeDtypeStruct((rows, m, p, p), BF),
        in_specs=[vmem] * 5 + [pl.BlockSpec(memory_space=pl.ANY)],
        out_specs=pl.BlockSpec(memory_space=pl.ANY),
        scratch_shapes=[
            pltpu.VMEM((per + 1, m, p, p), BF),
            pltpu.VMEM((rows, m, p, p), BF),
            pltpu.SMEM(coarse.shape, jnp.int32),
            pltpu.SemaphoreType.DMA,
            pltpu.SemaphoreType.DMA((rows,)),
        ],
        compiler_params=pltpu.CompilerParams(vmem_limit_bytes=38 * MIB),
        cost_estimate=pl.CostEstimate(
            flops=2 * rows * m * p**3, bytes_accessed=2 * rows * m * p * p, transcendentals=0
        ),
        name="fine_rows",
    )(coarse, c, following, right, u, after)


def shares_kernel(lows, n_row, n_col, c_ref, k_ref, f_ref, t_ref, own_ref, *refs):
    sends, w_v = refs[: n_row - 1], refs[-1]
    m, nv = t_ref.shape[:2]
    nc = k_ref.shape[0]
    s = two_terms(sum(dot(t_ref[q], c_ref[q], NT) for q in range(m)))
    each, half = nv // n_col, n_col // 2
    at = lax.broadcasted_iota(jnp.int32, (nv, nv), 1)
    block = lax.div(at, each)
    source = lax.bitwise_xor(lax.axis_index("col"), 2 * lax.rem(block, half) + lax.div(block, half))
    place = source * each + lax.rem(at, each)
    order = (place == lax.broadcasted_iota(jnp.int32, (nv, nv), 0)).astype(F32).astype(BF)
    s = jnp.concatenate([dot(order, s[:nv]), dot(order, s[nv:])], axis=0).astype(BF)
    for j in range(nc + 1):
        w_v[j] = folded_dot(s, k_ref[j] if j < nc else f_ref[0], NT)
    me = lax.axis_index("row")
    (own, spacing), width = lows
    own_ref[...] = w_v[pl.ds(me * own // spacing, width)]
    for n in range(1, n_row):
        other = lax.bitwise_xor(me, n)
        sends[n - 1][...] = w_v[pl.ds(other * own // spacing, width)].astype(BF)


def shares(lows, n_row, n_col, c, kb, following, t):
    nv, p = t.shape[1:]
    width = lows[1]
    vmem = pl.BlockSpec(memory_space=pltpu.VMEM)
    return pl.pallas_call(
        functools.partial(shares_kernel, lows, n_row, n_col),
        out_shape=[jax.ShapeDtypeStruct((width, nv, p), F32)]
        + [jax.ShapeDtypeStruct((width, nv, p), BF)] * (n_row - 1),
        in_specs=[vmem] * 4,
        out_specs=[vmem] * n_row,
        scratch_shapes=[pltpu.VMEM((kb.shape[0] + 1, nv, p), F32)],
        compiler_params=pltpu.CompilerParams(vmem_limit_bytes=16 * MIB),
        name="row_shares",
    )(c, kb, following, t)


def applied_kernel(lows, n_row, nc, spacing, coarse_ref, u_ref, own_ref, *refs):
    got = refs[: n_row - 1]
    out, w_v, coarse, csem = refs[-4:]
    (own, _), width = lows
    load = pltpu.make_async_copy(coarse_ref, coarse, csem)
    load.start()
    me = lax.axis_index("row")
    base_j = lax.axis_index("col") * nc + me * own // spacing
    base_k = lax.axis_index("col") * nc * spacing + me * own
    w = own_ref[...]
    for ref in got:
        w = w + ref[...].astype(F32)
    for i in range(width):
        w_v[i] = two_terms(w[i])
    load.wait()
    for t in range(own):
        at = jnp.clip(coarse[base_k + t] - base_j, 0, width - 1)
        out[t] = folded_dot(w_v[at], u_ref[me * own + t]).astype(BF)


def applied_rows(lows, n_row, nc, spacing, coarse, u, own_share, got):
    width, nv, p = own_share.shape
    vmem = pl.BlockSpec(memory_space=pltpu.VMEM)
    return pl.pallas_call(
        functools.partial(applied_kernel, lows, n_row, nc, spacing),
        out_shape=jax.ShapeDtypeStruct((lows[0][0], nv, p), BF),
        in_specs=[vmem] * (n_row + 2),
        out_specs=vmem,
        scratch_shapes=[
            pltpu.VMEM((width, 2 * nv, p), BF),
            pltpu.SMEM(coarse.shape, jnp.int32),
            pltpu.SemaphoreType.DMA,
        ],
        compiler_params=pltpu.CompilerParams(vmem_limit_bytes=24 * MIB),
        name="applied_rows",
    )(coarse, u, own_share, *got)


def swap(x, by):
    n = lax.axis_size("col")
    return lax.ppermute(x, "col", [(i, i ^ by) for i in range(n)])


def per_device(kb, u, c, trial, coarse):
    n_row, n_col = lax.axis_size("row"), lax.axis_size("col")
    nc, rows = kb.shape[0], u.shape[0]
    spacing = rows // nc
    own = rows // n_row
    width = max((r * own + own - 1) // spacing + 2 - r * own // spacing for r in range(n_row))
    lows = ((own, spacing), width)
    others = [swap(trial, by) for by in range(2, n_col, 2)]
    c, blocks, u, trial, coarse, first, right = ready(spacing, *[pltpu.with_memory_space_constraint(x, pltpu.HBM) for x in (c, kb, u, trial, coarse)])
    half = jnp.concatenate([trial] + others, axis=1)
    full = jnp.concatenate([half, swap(half, 1)], axis=1)
    following = lax.ppermute(first, "col", [(i + 1, i) for i in range(n_col - 1)])
    own_share, *sends = shares(lows, n_row, n_col, c, blocks, following, full)
    got = [lax.ppermute(x, "row", [(i, i ^ (n + 1)) for i in range(n_row)]) for n, x in enumerate(sends)]
    fine = fine_rows(spacing, coarse, c, following, right, u, own_share)
    applied = applied_rows(lows, n_row, nc, spacing, coarse, u, own_share, got)
    return fine, applied


def solution(mesh):
    in_specs = (
        P("col", "row", None, None),
        P("col", None, None),
        P("row", None, None),
        P("row", "col", None),
        P(),
    )
    out_specs = (P("col", "row", None, None), P(("col", "row"), None, None))
    return jax.shard_map(
        per_device, mesh=mesh, in_specs=in_specs, out_specs=out_specs, check_vma=False
    )
```

```python
import functools

import jax
import jax.numpy as jnp
from jax import lax
from jax.experimental import pallas as pl
from jax.experimental.pallas import tpu as pltpu
from jax.sharding import PartitionSpec as P

BF = jnp.bfloat16
F32 = jnp.float32
MIB = 1024 * 1024
NT = (((1,), (1,)), ((), ()))
NN = (((1,), (0,)), ((), ()))


def dot(x, y, dims=NN):
    return lax.dot_general(x, y, dims, preferred_element_type=F32)


def two_terms(x):
    high = x.astype(BF)
    low = (x - high.astype(F32)).astype(BF)
    return jnp.concatenate([high, low], axis=0)


def folded_dot(x, y, dims=NN):
    z = dot(x, y, dims)
    half = z.shape[0] // 2
    return z[:half] + z[half:]


def ready_kernel(k_hbm, t_hbm, coarse_hbm, first_v, t_v, coarse_v, ksem, tsem, csem):
    loads = [
        pltpu.make_async_copy(k_hbm.at[0], first_v, ksem),
        pltpu.make_async_copy(t_hbm, t_v, tsem),
        pltpu.make_async_copy(coarse_hbm, coarse_v, csem),
    ]
    for load in loads:
        load.start()
    for load in loads:
        load.wait()


def ready(kb, trial, coarse, work):
    vmem = pl.BlockSpec(memory_space=pltpu.VMEM)
    held = [pltpu.with_memory_space_constraint(x, pltpu.HBM) for x in (kb, trial, coarse)]
    return pl.pallas_call(
        ready_kernel,
        out_shape=[
            jax.ShapeDtypeStruct(kb.shape[1:], BF),
            jax.ShapeDtypeStruct(trial.shape, BF),
            jax.ShapeDtypeStruct(coarse.shape, jnp.int32),
        ],
        in_specs=[pl.BlockSpec(memory_space=pl.ANY)] * 3,
        out_specs=[vmem] * 3,
        scratch_shapes=[pltpu.SemaphoreType.DMA] * 3,
        compiler_params=pltpu.CompilerParams(vmem_limit_bytes=32 * MIB),
        cost_estimate=pl.CostEstimate(flops=work, bytes_accessed=2 * kb.size, transcendentals=0),
        name="ready",
    )(*held)


def right_kernel(c_ref, k_ref, _, r_ref):
    for j in range(k_ref.shape[0]):
        for q in range(c_ref.shape[0]):
            r_ref[j, q] = dot(k_ref[j, 0], c_ref[q]).astype(BF)


def right_blocks(c, kb, after):
    nc, _, p, _ = kb.shape
    m = c.shape[0]
    vmem = pl.BlockSpec(memory_space=pltpu.VMEM)
    return pl.pallas_call(
        right_kernel,
        out_shape=jax.ShapeDtypeStruct((nc, m, p, p), BF),
        in_specs=[vmem] * 2 + [pl.BlockSpec(memory_space=pl.ANY)],
        out_specs=vmem,
        compiler_params=pltpu.CompilerParams(vmem_limit_bytes=32 * MIB),
        cost_estimate=pl.CostEstimate(flops=2 * nc * m * p**3, bytes_accessed=0, transcendentals=0),
        name="right_blocks",
    )(c, kb, after)


def rows_kernel(spacing, per, coarse_ref, c_ref, f_ref, r_ref, u_ref, _, out, r_v, o_v, coarse, csem, osem):
    nc, m = r_ref.shape[:2]
    base_j = lax.axis_index("col") * nc
    base_k = lax.axis_index("col") * nc * spacing
    load = pltpu.make_async_copy(coarse_ref, coarse, csem)
    load.start()

    def write(k):
        return pltpu.make_async_copy(o_v.at[k], out.at[k], osem.at[k])

    def rows(i, tail):
        for t in range(per * spacing):
            k = i * spacing + t
            at = coarse[base_k + k] - base_j
            ut = u_ref[k].T
            for q in range(m):
                if tail:
                    block = r_v[jnp.clip(at - (nc - per), 0, per), q]
                else:
                    block = r_ref[jnp.clip(at, 0, nc - 1), q]
                o_v[k, q] = dot(ut, block).astype(BF)
            write(k).start()

    for q in range(m):
        r_v[per, q] = dot(f_ref[0], c_ref[q]).astype(BF)
    for j in range(per):
        r_v[j] = r_ref[nc - per + j]
    load.wait()

    def step(n, carry):
        rows(n * per, False)
        return carry

    lax.fori_loop(0, nc // per - 1, step, 0)
    rows(nc - per, True)
    for k in range(nc * spacing):
        write(k).wait()


def fine_rows(spacing, coarse, c, following, right, u, after):
    rows, p, _ = u.shape
    nc, m = right.shape[:2]
    per = 2 if nc % 2 == 0 else 1
    vmem = pl.BlockSpec(memory_space=pltpu.VMEM)
    return pl.pallas_call(
        functools.partial(rows_kernel, spacing, per),
        out_shape=jax.ShapeDtypeStruct((rows, m, p, p), BF),
        in_specs=[vmem] * 5 + [pl.BlockSpec(memory_space=pl.ANY)],
        out_specs=pl.BlockSpec(memory_space=pl.ANY),
        scratch_shapes=[
            pltpu.VMEM((per + 1, m, p, p), BF),
            pltpu.VMEM((rows, m, p, p), BF),
            pltpu.SMEM(coarse.shape, jnp.int32),
            pltpu.SemaphoreType.DMA,
            pltpu.SemaphoreType.DMA((rows,)),
        ],
        compiler_params=pltpu.CompilerParams(vmem_limit_bytes=38 * MIB),
        cost_estimate=pl.CostEstimate(
            flops=2 * rows * m * p**3, bytes_accessed=2 * rows * m * p * p, transcendentals=0
        ),
        name="fine_rows",
    )(coarse, c, following, right, u, after)


def shares_kernel(lows, n_row, n_col, c_ref, k_ref, f_ref, t_ref, own_ref, *refs):
    sends, w_v = refs[: n_row - 1], refs[-1]
    m, nv = t_ref.shape[:2]
    nc = k_ref.shape[0]
    s = two_terms(sum(dot(t_ref[q], c_ref[q], NT) for q in range(m)))
    each, half = nv // n_col, n_col // 2
    at = lax.broadcasted_iota(jnp.int32, (nv, nv), 1)
    block = lax.div(at, each)
    source = lax.bitwise_xor(
        lax.axis_index("col"), lax.rem(n_col - 2 * lax.rem(block, half), n_col) + lax.div(block, half)
    )
    place = source * each + lax.rem(at, each)
    order = (place == lax.broadcasted_iota(jnp.int32, (nv, nv), 0)).astype(F32).astype(BF)
    s = jnp.concatenate([dot(order, s[:nv]), dot(order, s[nv:])], axis=0).astype(BF)
    for j in range(nc + 1):
        w_v[j] = folded_dot(s, k_ref[j, 0] if j < nc else f_ref[0], NT)
    me = lax.axis_index("row")
    (own, spacing), width = lows
    own_ref[...] = w_v[pl.ds(me * own // spacing, width)]
    for n in range(1, n_row):
        other = lax.bitwise_xor(me, n)
        sends[n - 1][...] = w_v[pl.ds(other * own // spacing, width)].astype(BF)


def shares(lows, n_row, n_col, c, kb, following, t):
    nv, p = t.shape[1:]
    width = lows[1]
    vmem = pl.BlockSpec(memory_space=pltpu.VMEM)
    return pl.pallas_call(
        functools.partial(shares_kernel, lows, n_row, n_col),
        out_shape=[jax.ShapeDtypeStruct((width, nv, p), F32)]
        + [jax.ShapeDtypeStruct((width, nv, p), BF)] * (n_row - 1),
        in_specs=[vmem] * 4,
        out_specs=[vmem] * n_row,
        scratch_shapes=[pltpu.VMEM((kb.shape[0] + 1, nv, p), F32)],
        compiler_params=pltpu.CompilerParams(vmem_limit_bytes=16 * MIB),
        name="row_shares",
    )(c, kb, following, t)


def applied_kernel(lows, n_row, nc, spacing, coarse_ref, u_ref, own_ref, *refs):
    got = refs[: n_row - 1]
    out, w_v, o_v, coarse, csem, osem = refs[-6:]
    (own, _), width = lows
    load = pltpu.make_async_copy(coarse_ref, coarse, csem)
    load.start()
    me = lax.axis_index("row")
    base_j = lax.axis_index("col") * nc + me * own // spacing
    base_k = lax.axis_index("col") * nc * spacing + me * own
    w = own_ref[...]
    for ref in got:
        w = w + ref[...].astype(F32)
    for i in range(width):
        w_v[i] = two_terms(w[i])
    load.wait()
    part = min(4, own)

    def write(t):
        here = pl.ds(t, part)
        return pltpu.make_async_copy(o_v.at[here], out.at[here], osem.at[t])

    for t in range(own):
        at = jnp.clip(coarse[base_k + t] - base_j, 0, width - 1)
        o_v[t] = folded_dot(w_v[at], u_ref[me * own + t]).astype(BF)
        if (t + 1) % part == 0:
            write(t + 1 - part).start()
    for t in range(0, own, part):
        write(t).wait()


def applied_rows(lows, n_row, nc, spacing, coarse, u, own_share, got):
    width, nv, p = own_share.shape
    vmem = pl.BlockSpec(memory_space=pltpu.VMEM)
    return pl.pallas_call(
        functools.partial(applied_kernel, lows, n_row, nc, spacing),
        out_shape=jax.ShapeDtypeStruct((lows[0][0], nv, p), BF),
        in_specs=[vmem] * (n_row + 2),
        out_specs=pl.BlockSpec(memory_space=pl.ANY),
        scratch_shapes=[
            pltpu.VMEM((width, 2 * nv, p), BF),
            pltpu.VMEM((lows[0][0], nv, p), BF),
            pltpu.SMEM(coarse.shape, jnp.int32),
            pltpu.SemaphoreType.DMA,
            pltpu.SemaphoreType.DMA((lows[0][0],)),
        ],
        compiler_params=pltpu.CompilerParams(vmem_limit_bytes=24 * MIB),
        name="applied_rows",
    )(coarse, u, own_share, *got)


def swap(x, by):
    n = lax.axis_size("col")
    return lax.ppermute(x, "col", [(i, i ^ by) for i in range(n)])


def per_device(kb, u, c, trial, coarse):
    n_row, n_col = lax.axis_size("row"), lax.axis_size("col")
    nc, rows = kb.shape[0], u.shape[0]
    spacing = rows // nc
    own = rows // n_row
    width = max((r * own + own - 1) // spacing + 2 - r * own // spacing for r in range(n_row))
    lows = ((own, spacing), width)
    others = [swap(trial, by) for by in range(n_col - 2, 0, -2)]
    work = 12 * nc * c.shape[0] * c.shape[1] ** 3
    first, trial, coarse = ready(kb, trial, coarse, work)
    half = jnp.concatenate([trial] + others, axis=1)
    right = right_blocks(c, kb, half)
    full = jnp.concatenate([half, swap(half, 1)], axis=1)
    following = lax.ppermute(first, "col", [(i + 1, i) for i in range(n_col - 1)])
    own_share, *sends = shares(lows, n_row, n_col, c, kb, following, full)
    got = [lax.ppermute(x, "row", [(i, i ^ (n + 1)) for i in range(n_row)]) for n, x in enumerate(sends)]
    fine = fine_rows(spacing, coarse, c, following, right, u, own_share)
    applied = applied_rows(lows, n_row, nc, spacing, coarse, u, own_share, got)
    return fine, applied


def solution(mesh):
    in_specs = (
        P("col", "row", None, None),
        P("col", None, None),
        P("row", None, None),
        P("row", "col", None),
        P(),
    )
    out_specs = (P("col", "row", None, None), P(("col", "row"), None, None))
    return jax.shard_map(
        per_device, mesh=mesh, in_specs=in_specs, out_specs=out_specs, check_vma=False
    )
```

```python
import functools

import jax
import jax.numpy as jnp
from jax import lax
from jax.experimental import pallas as pl
from jax.experimental.pallas import tpu as pltpu
from jax.sharding import PartitionSpec as P

BF = jnp.bfloat16
F32 = jnp.float32
MIB = 1024 * 1024
NT = (((1,), (1,)), ((), ()))
NN = (((1,), (0,)), ((), ()))


def dot(x, y, dims=NN):
    return lax.dot_general(x, y, dims, preferred_element_type=F32)


def two_terms(x):
    high = x.astype(BF)
    low = (x - high.astype(F32)).astype(BF)
    return jnp.concatenate([high, low], axis=0)


def folded_dot(x, y, dims=NN):
    z = dot(x, y, dims)
    half = z.shape[0] // 2
    return z[:half] + z[half:]


def ready_kernel(k_hbm, t_hbm, coarse_hbm, first_v, t_v, coarse_v, ksem, tsem, csem):
    loads = [
        pltpu.make_async_copy(k_hbm.at[0], first_v, ksem),
        pltpu.make_async_copy(t_hbm, t_v, tsem),
        pltpu.make_async_copy(coarse_hbm, coarse_v, csem),
    ]
    for load in loads:
        load.start()
    for load in loads:
        load.wait()


def ready(kb, trial, coarse, work):
    vmem = pl.BlockSpec(memory_space=pltpu.VMEM)
    held = [pltpu.with_memory_space_constraint(x, pltpu.HBM) for x in (kb, trial, coarse)]
    return pl.pallas_call(
        ready_kernel,
        out_shape=[
            jax.ShapeDtypeStruct(kb.shape[1:], BF),
            jax.ShapeDtypeStruct(trial.shape, BF),
            jax.ShapeDtypeStruct(coarse.shape, jnp.int32),
        ],
        in_specs=[pl.BlockSpec(memory_space=pl.ANY)] * 3,
        out_specs=[vmem] * 3,
        scratch_shapes=[pltpu.SemaphoreType.DMA] * 3,
        compiler_params=pltpu.CompilerParams(vmem_limit_bytes=32 * MIB),
        cost_estimate=pl.CostEstimate(flops=work, bytes_accessed=2 * kb.size, transcendentals=0),
        name="ready",
    )(*held)


def right_kernel(c_ref, k_ref, _, r_ref):
    for j in range(k_ref.shape[0]):
        for q in range(c_ref.shape[0]):
            r_ref[j, q] = dot(k_ref[j, 0], c_ref[q]).astype(BF)


def right_blocks(c, kb, after):
    nc, _, p, _ = kb.shape
    m = c.shape[0]
    vmem = pl.BlockSpec(memory_space=pltpu.VMEM)
    return pl.pallas_call(
        right_kernel,
        out_shape=jax.ShapeDtypeStruct((nc + 1, m, p, p), BF),
        in_specs=[vmem] * 2 + [pl.BlockSpec(memory_space=pl.ANY)],
        out_specs=vmem,
        compiler_params=pltpu.CompilerParams(vmem_limit_bytes=32 * MIB),
        cost_estimate=pl.CostEstimate(flops=2 * nc * m * p**3, bytes_accessed=0, transcendentals=0),
        name="right_blocks",
    )(c, kb, after)


def rows_kernel(spacing, coarse_ref, c_ref, f_ref, _, u_ref, __, out, r_ref, o_v, coarse, csem, osem):
    nc, m = r_ref.shape[0] - 1, r_ref.shape[1]
    base_j = lax.axis_index("col") * nc
    base_k = lax.axis_index("col") * nc * spacing
    per = min(2, nc) * spacing
    load = pltpu.make_async_copy(coarse_ref, coarse, csem)
    load.start()

    def write(k):
        return pltpu.make_async_copy(o_v.at[k], out.at[k], osem.at[k])

    load.wait()

    def step(i, carry):
        for t in range(per):
            k = i * per + t
            at = jnp.clip(coarse[base_k + k] - base_j, 0, nc)
            ut = u_ref[k].T
            for q in range(m):
                o_v[k, q] = dot(ut, r_ref[at, q]).astype(BF)
            write(k).start()

        @pl.when(i == 0)
        def _():
            for q in range(m):
                r_ref[nc, q] = dot(f_ref[0], c_ref[q]).astype(BF)

        return carry

    lax.fori_loop(0, nc * spacing // per, step, 0)
    for k in range(nc * spacing):
        write(k).wait()


def fine_rows(spacing, coarse, c, following, right, u, after):
    rows, p, _ = u.shape
    m = right.shape[1]
    vmem = pl.BlockSpec(memory_space=pltpu.VMEM)
    return pl.pallas_call(
        functools.partial(rows_kernel, spacing),
        out_shape=[jax.ShapeDtypeStruct((rows, m, p, p), BF), jax.ShapeDtypeStruct(right.shape, BF)],
        in_specs=[vmem] * 5 + [pl.BlockSpec(memory_space=pl.ANY)],
        out_specs=[pl.BlockSpec(memory_space=pl.ANY), vmem],
        scratch_shapes=[
            pltpu.VMEM((rows, m, p, p), BF),
            pltpu.SMEM(coarse.shape, jnp.int32),
            pltpu.SemaphoreType.DMA,
            pltpu.SemaphoreType.DMA((rows,)),
        ],
        input_output_aliases={3: 1},
        compiler_params=pltpu.CompilerParams(vmem_limit_bytes=38 * MIB),
        cost_estimate=pl.CostEstimate(
            flops=2 * rows * m * p**3, bytes_accessed=2 * rows * m * p * p, transcendentals=0
        ),
        name="fine_rows",
    )(coarse, c, following, right, u, after)[0]


def shares_kernel(lows, n_row, n_col, c_ref, k_ref, f_ref, t_ref, own_ref, *refs):
    sends, w_v = refs[: n_row - 1], refs[-1]
    m, nv = t_ref.shape[:2]
    nc = k_ref.shape[0]
    s = two_terms(sum(dot(t_ref[q], c_ref[q], NT) for q in range(m)))
    each, half = nv // n_col, n_col // 2
    at = lax.broadcasted_iota(jnp.int32, (nv, nv), 1)
    block = lax.div(at, each)
    source = lax.bitwise_xor(
        lax.axis_index("col"), lax.rem(n_col - 2 * lax.rem(block, half), n_col) + lax.div(block, half)
    )
    place = source * each + lax.rem(at, each)
    order = (place == lax.broadcasted_iota(jnp.int32, (nv, nv), 0)).astype(F32).astype(BF)
    s = jnp.concatenate([dot(order, s[:nv]), dot(order, s[nv:])], axis=0).astype(BF)
    for j in range(nc + 1):
        w_v[j] = folded_dot(s, k_ref[j, 0] if j < nc else f_ref[0], NT)
    me = lax.axis_index("row")
    (own, spacing), width = lows
    own_ref[...] = w_v[pl.ds(me * own // spacing, width)]
    for n in range(1, n_row):
        other = lax.bitwise_xor(me, n)
        sends[n - 1][...] = w_v[pl.ds(other * own // spacing, width)].astype(BF)


def shares(lows, n_row, n_col, c, kb, following, t):
    nv, p = t.shape[1:]
    width = lows[1]
    vmem = pl.BlockSpec(memory_space=pltpu.VMEM)
    return pl.pallas_call(
        functools.partial(shares_kernel, lows, n_row, n_col),
        out_shape=[jax.ShapeDtypeStruct((width, nv, p), F32)]
        + [jax.ShapeDtypeStruct((width, nv, p), BF)] * (n_row - 1),
        in_specs=[vmem] * 4,
        out_specs=[vmem] * n_row,
        scratch_shapes=[pltpu.VMEM((kb.shape[0] + 1, nv, p), F32)],
        compiler_params=pltpu.CompilerParams(vmem_limit_bytes=16 * MIB),
        name="row_shares",
    )(c, kb, following, t)


def applied_kernel(lows, n_row, nc, spacing, coarse_ref, u_ref, own_ref, *refs):
    got = refs[: n_row - 1]
    out, w_v, o_v, coarse, csem, osem = refs[-6:]
    (own, _), width = lows
    load = pltpu.make_async_copy(coarse_ref, coarse, csem)
    load.start()
    me = lax.axis_index("row")
    base_j = lax.axis_index("col") * nc + me * own // spacing
    base_k = lax.axis_index("col") * nc * spacing + me * own
    w = own_ref[...]
    for ref in got:
        w = w + ref[...].astype(F32)
    for i in range(width):
        w_v[i] = two_terms(w[i])
    load.wait()
    part = min(4, own)

    def write(t):
        here = pl.ds(t, part)
        return pltpu.make_async_copy(o_v.at[here], out.at[here], osem.at[t])

    for t in range(own):
        at = jnp.clip(coarse[base_k + t] - base_j, 0, width - 1)
        o_v[t] = folded_dot(w_v[at], u_ref[me * own + t]).astype(BF)
        if (t + 1) % part == 0:
            write(t + 1 - part).start()
    for t in range(0, own, part):
        write(t).wait()


def applied_rows(lows, n_row, nc, spacing, coarse, u, own_share, got):
    width, nv, p = own_share.shape
    vmem = pl.BlockSpec(memory_space=pltpu.VMEM)
    return pl.pallas_call(
        functools.partial(applied_kernel, lows, n_row, nc, spacing),
        out_shape=jax.ShapeDtypeStruct((lows[0][0], nv, p), BF),
        in_specs=[vmem] * (n_row + 2),
        out_specs=pl.BlockSpec(memory_space=pl.ANY),
        scratch_shapes=[
            pltpu.VMEM((width, 2 * nv, p), BF),
            pltpu.VMEM((lows[0][0], nv, p), BF),
            pltpu.SMEM(coarse.shape, jnp.int32),
            pltpu.SemaphoreType.DMA,
            pltpu.SemaphoreType.DMA((lows[0][0],)),
        ],
        compiler_params=pltpu.CompilerParams(vmem_limit_bytes=24 * MIB),
        name="applied_rows",
    )(coarse, u, own_share, *got)


def swap(x, by):
    n = lax.axis_size("col")
    return lax.ppermute(x, "col", [(i, i ^ by) for i in range(n)])


def per_device(kb, u, c, trial, coarse):
    n_row, n_col = lax.axis_size("row"), lax.axis_size("col")
    nc, rows = kb.shape[0], u.shape[0]
    spacing = rows // nc
    own = rows // n_row
    width = max((r * own + own - 1) // spacing + 2 - r * own // spacing for r in range(n_row))
    lows = ((own, spacing), width)
    others = [swap(trial, by) for by in range(n_col - 2, 0, -2)]
    work = 12 * nc * c.shape[0] * c.shape[1] ** 3
    first, trial, coarse = ready(kb, trial, coarse, work)
    half = jnp.concatenate([trial] + others, axis=1)
    right = right_blocks(c, kb, half)
    full = jnp.concatenate([half, swap(half, 1)], axis=1)
    following = lax.ppermute(first, "col", [(i + 1, i) for i in range(n_col - 1)])
    own_share, *sends = shares(lows, n_row, n_col, c, kb, following, full)
    got = [lax.ppermute(x, "row", [(i, i ^ (n + 1)) for i in range(n_row)]) for n, x in enumerate(sends)]
    fine = fine_rows(spacing, coarse, c, following, right, u, own_share)
    applied = applied_rows(lows, n_row, nc, spacing, coarse, u, own_share, got)
    return fine, applied


def solution(mesh):
    in_specs = (
        P("col", "row", None, None),
        P("col", None, None),
        P("row", None, None),
        P("row", "col", None),
        P(),
    )
    out_specs = (P("col", "row", None, None), P(("col", "row"), None, None))
    return jax.shard_map(
        per_device, mesh=mesh, in_specs=in_specs, out_specs=out_specs, check_vma=False
    )
```

```python
import functools

import jax
import jax.numpy as jnp
from jax import lax
from jax.experimental import pallas as pl
from jax.experimental.pallas import tpu as pltpu
from jax.sharding import PartitionSpec as P

BF = jnp.bfloat16
F32 = jnp.float32
MIB = 1024 * 1024
NT = (((1,), (1,)), ((), ()))
NN = (((1,), (0,)), ((), ()))


def dot(x, y, dims=NN):
    return lax.dot_general(x, y, dims, preferred_element_type=F32)


def two_terms(x):
    high = x.astype(BF)
    low = (x - high.astype(F32)).astype(BF)
    return jnp.concatenate([high, low], axis=0)


def folded_dot(x, y, dims=NN):
    z = dot(x, y, dims)
    half = z.shape[0] // 2
    return z[:half] + z[half:]


def ready_kernel(k_hbm, t_hbm, coarse_hbm, first_v, t_v, coarse_v, ksem, tsem, csem):
    loads = [
        pltpu.make_async_copy(k_hbm.at[0], first_v, ksem),
        pltpu.make_async_copy(t_hbm, t_v, tsem),
        pltpu.make_async_copy(coarse_hbm, coarse_v, csem),
    ]
    for load in loads:
        load.start()
    for load in loads:
        load.wait()


def ready(kb, trial, coarse, work):
    vmem = pl.BlockSpec(memory_space=pltpu.VMEM)
    held = [pltpu.with_memory_space_constraint(x, pltpu.HBM) for x in (kb, trial, coarse)]
    return pl.pallas_call(
        ready_kernel,
        out_shape=[
            jax.ShapeDtypeStruct(kb.shape[1:], BF),
            jax.ShapeDtypeStruct(trial.shape, BF),
            jax.ShapeDtypeStruct(coarse.shape, jnp.int32),
        ],
        in_specs=[pl.BlockSpec(memory_space=pl.ANY)] * 3,
        out_specs=[vmem] * 3,
        scratch_shapes=[pltpu.SemaphoreType.DMA] * 3,
        compiler_params=pltpu.CompilerParams(vmem_limit_bytes=32 * MIB),
        cost_estimate=pl.CostEstimate(flops=work, bytes_accessed=2 * kb.size, transcendentals=0),
        name="ready",
    )(*held)


def right_kernel(c_ref, k_ref, _, r_ref):
    for j in range(k_ref.shape[0]):
        for q in range(c_ref.shape[0]):
            r_ref[j, q] = dot(k_ref[j, 0], c_ref[q]).astype(BF)


def right_blocks(c, kb, after):
    nc, _, p, _ = kb.shape
    m = c.shape[0]
    vmem = pl.BlockSpec(memory_space=pltpu.VMEM)
    return pl.pallas_call(
        right_kernel,
        out_shape=jax.ShapeDtypeStruct((nc, m, p, p), BF),
        in_specs=[vmem] * 2 + [pl.BlockSpec(memory_space=pl.ANY)],
        out_specs=vmem,
        compiler_params=pltpu.CompilerParams(vmem_limit_bytes=32 * MIB),
        cost_estimate=pl.CostEstimate(flops=2 * nc * m * p**3, bytes_accessed=0, transcendentals=0),
        name="right_blocks",
    )(c, kb, after)


def rows_kernel(spacing, per, coarse_ref, c_ref, f_ref, r_ref, u_ref, _, out, r_v, o_v, coarse, csem, osem):
    nc, m = r_ref.shape[:2]
    base_j = lax.axis_index("col") * nc
    base_k = lax.axis_index("col") * nc * spacing
    load = pltpu.make_async_copy(coarse_ref, coarse, csem)
    load.start()

    def write(k):
        return pltpu.make_async_copy(o_v.at[k], out.at[k], osem.at[k])

    def rows(i, tail):
        for t in range(per * spacing):
            k = i * spacing + t
            at = coarse[base_k + k] - base_j
            ut = u_ref[k].T
            for q in range(m):
                if tail:
                    block = r_v[jnp.clip(at - (nc - per), 0, per), q]
                else:
                    block = r_ref[jnp.clip(at, 0, nc - 1), q]
                o_v[k, q] = dot(ut, block).astype(BF)
            write(k).start()

    for q in range(m):
        r_v[per, q] = dot(f_ref[0], c_ref[q]).astype(BF)
    for j in range(per):
        r_v[j] = r_ref[nc - per + j]
    load.wait()

    def step(n, carry):
        rows(n * per, False)
        return carry

    lax.fori_loop(0, nc // per - 1, step, 0)
    rows(nc - per, True)
    for k in range(nc * spacing):
        write(k).wait()


def fine_rows(spacing, coarse, c, following, right, u, after):
    rows, p, _ = u.shape
    nc, m = right.shape[:2]
    per = 2 if nc % 2 == 0 else 1
    vmem = pl.BlockSpec(memory_space=pltpu.VMEM)
    return pl.pallas_call(
        functools.partial(rows_kernel, spacing, per),
        out_shape=jax.ShapeDtypeStruct((rows, m, p, p), BF),
        in_specs=[vmem] * 5 + [pl.BlockSpec(memory_space=pl.ANY)],
        out_specs=pl.BlockSpec(memory_space=pl.ANY),
        scratch_shapes=[
            pltpu.VMEM((per + 1, m, p, p), BF),
            pltpu.VMEM((rows, m, p, p), BF),
            pltpu.SMEM(coarse.shape, jnp.int32),
            pltpu.SemaphoreType.DMA,
            pltpu.SemaphoreType.DMA((rows,)),
        ],
        compiler_params=pltpu.CompilerParams(vmem_limit_bytes=38 * MIB),
        cost_estimate=pl.CostEstimate(
            flops=2 * rows * m * p**3, bytes_accessed=2 * rows * m * p * p, transcendentals=0
        ),
        name="fine_rows",
    )(coarse, c, following, right, u, after)


def shares_kernel(lows, n_row, n_col, c_ref, k_ref, f_ref, t_ref, own_ref, *refs):
    sends, w_v = refs[: n_row - 1], refs[-1]
    m, nv = t_ref.shape[:2]
    nc = k_ref.shape[0]
    t = jnp.concatenate([t_ref[q] for q in range(m)], axis=1)
    s = two_terms(dot(t, jnp.concatenate([c_ref[q] for q in range(m)], axis=1), NT))
    each, half = nv // n_col, n_col // 2
    at = lax.broadcasted_iota(jnp.int32, (nv, nv), 1)
    block = lax.div(at, each)
    source = lax.bitwise_xor(
        lax.axis_index("col"), lax.rem(n_col - 2 * lax.rem(block, half), n_col) + lax.div(block, half)
    )
    place = source * each + lax.rem(at, each)
    order = (place == lax.broadcasted_iota(jnp.int32, (nv, nv), 0)).astype(F32).astype(BF)
    s = dot(order, jnp.concatenate([s[:nv], s[nv:]], axis=1)).astype(BF)
    s = jnp.concatenate([s[:, : s.shape[1] // 2], s[:, s.shape[1] // 2 :]], axis=0)
    for j in range(nc + 1):
        w_v[j] = folded_dot(s, k_ref[j, 0] if j < nc else f_ref[0], NT)
    me = lax.axis_index("row")
    (own, spacing), width = lows
    own_ref[...] = w_v[pl.ds(me * own // spacing, width)]
    for n in range(1, n_row):
        other = lax.bitwise_xor(me, n)
        sends[n - 1][...] = w_v[pl.ds(other * own // spacing, width)].astype(BF)


def shares(lows, n_row, n_col, c, kb, following, t):
    nv, p = t.shape[1:]
    width = lows[1]
    vmem = pl.BlockSpec(memory_space=pltpu.VMEM)
    return pl.pallas_call(
        functools.partial(shares_kernel, lows, n_row, n_col),
        out_shape=[jax.ShapeDtypeStruct((width, nv, p), F32)]
        + [jax.ShapeDtypeStruct((width, nv, p), BF)] * (n_row - 1),
        in_specs=[vmem] * 4,
        out_specs=[vmem] * n_row,
        scratch_shapes=[pltpu.VMEM((kb.shape[0] + 1, nv, p), F32)],
        compiler_params=pltpu.CompilerParams(vmem_limit_bytes=16 * MIB),
        name="row_shares",
    )(c, kb, following, t)


def applied_kernel(lows, n_row, nc, spacing, coarse_ref, u_ref, own_ref, *refs):
    got = refs[: n_row - 1]
    out, w_v, o_v, coarse, csem, osem = refs[-6:]
    (own, _), width = lows
    load = pltpu.make_async_copy(coarse_ref, coarse, csem)
    load.start()
    me = lax.axis_index("row")
    base_j = lax.axis_index("col") * nc + me * own // spacing
    base_k = lax.axis_index("col") * nc * spacing + me * own
    w = own_ref[...]
    for ref in got:
        w = w + ref[...].astype(F32)
    for i in range(width):
        w_v[i] = two_terms(w[i])
    load.wait()
    part = min(4, own)

    def write(t):
        here = pl.ds(t, part)
        return pltpu.make_async_copy(o_v.at[here], out.at[here], osem.at[t])

    for t in range(own):
        at = jnp.clip(coarse[base_k + t] - base_j, 0, width - 1)
        o_v[t] = folded_dot(w_v[at], u_ref[me * own + t]).astype(BF)
        if (t + 1) % part == 0:
            write(t + 1 - part).start()
    for t in range(0, own, part):
        write(t).wait()


def applied_rows(lows, n_row, nc, spacing, coarse, u, own_share, got):
    width, nv, p = own_share.shape
    vmem = pl.BlockSpec(memory_space=pltpu.VMEM)
    return pl.pallas_call(
        functools.partial(applied_kernel, lows, n_row, nc, spacing),
        out_shape=jax.ShapeDtypeStruct((lows[0][0], nv, p), BF),
        in_specs=[vmem] * (n_row + 2),
        out_specs=pl.BlockSpec(memory_space=pl.ANY),
        scratch_shapes=[
            pltpu.VMEM((width, 2 * nv, p), BF),
            pltpu.VMEM((lows[0][0], nv, p), BF),
            pltpu.SMEM(coarse.shape, jnp.int32),
            pltpu.SemaphoreType.DMA,
            pltpu.SemaphoreType.DMA((lows[0][0],)),
        ],
        compiler_params=pltpu.CompilerParams(vmem_limit_bytes=24 * MIB),
        name="applied_rows",
    )(coarse, u, own_share, *got)


def swap(x, by):
    n = lax.axis_size("col")
    return lax.ppermute(x, "col", [(i, i ^ by) for i in range(n)])


def per_device(kb, u, c, trial, coarse):
    n_row, n_col = lax.axis_size("row"), lax.axis_size("col")
    nc, rows = kb.shape[0], u.shape[0]
    spacing = rows // nc
    own = rows // n_row
    width = max((r * own + own - 1) // spacing + 2 - r * own // spacing for r in range(n_row))
    lows = ((own, spacing), width)
    others = [swap(trial, by) for by in range(n_col - 2, 0, -2)]
    work = 12 * nc * c.shape[0] * c.shape[1] ** 3
    first, trial, coarse = ready(kb, trial, coarse, work)
    half = jnp.concatenate([trial] + others, axis=1)
    right = right_blocks(c, kb, half)
    full = jnp.concatenate([half, swap(half, 1)], axis=1)
    following = lax.ppermute(first, "col", [(i + 1, i) for i in range(n_col - 1)])
    own_share, *sends = shares(lows, n_row, n_col, c, kb, following, full)
    got = [lax.ppermute(x, "row", [(i, i ^ (n + 1)) for i in range(n_row)]) for n, x in enumerate(sends)]
    fine = fine_rows(spacing, coarse, c, following, right, u, own_share)
    applied = applied_rows(lows, n_row, nc, spacing, coarse, u, own_share, got)
    return fine, applied


def solution(mesh):
    in_specs = (
        P("col", "row", None, None),
        P("col", None, None),
        P("row", None, None),
        P("row", "col", None),
        P(),
    )
    out_specs = (P("col", "row", None, None), P(("col", "row"), None, None))
    return jax.shard_map(
        per_device, mesh=mesh, in_specs=in_specs, out_specs=out_specs, check_vma=False
    )
```
